32 devices in a mesh: req: 16 (over z, x, core), ch: 2 (over y).
Axes of the slice: x: 2, y: 2, z: 4, core: 2. Of those that a mesh axis runs over, the one named last changes fastest.
Arguments:
- tokens: bfloat16 [32, 4096], P('req', 'ch'), may hold values from -80 to 80
- attn_gain: float32 [4096], P('ch'), may hold values from 0.1 to 1.9
- w_query: bfloat16 [4096, 4096], P('ch', 'req'), may hold values from -0.09375 to 0.09375
- w_keyval: bfloat16 [4096, 512], P('ch', 'req'), may hold values from -0.09375 to 0.09375
- cache: bfloat16 [2, 32, 256, 2048], P(None, 'req', 'ch'), may hold values from -70 to 70
- lengths: int32 [32], P('req'), may hold values from 1 to 2047, as said below
- write_pos: int32 [32], P('req'), may hold values from 0 to 2047
- w_out: bfloat16 [4096, 4096], P('ch', 'req'), may hold values from -0.09375 to 0.09375
- mlp_gain: float32 [4096], P('ch'), may hold values from 0.1 to 1.9
- w_gate_up: bfloat16 [4096, 24576], P('ch', 'req'), may hold values from -0.09375 to 0.09375
- w_down: bfloat16 [12288, 4096], P('req', 'ch'), may hold values from -0.0546875 to 0.0546875
Outputs:
- layer_out: bfloat16 [32, 4096], P('req', 'ch')
- kv_new: bfloat16 [32, 512], P('req', 'ch')
The draws below stay inside these ranges and needn't reach their ends.
Inputs may be any that keep to these rules, and one draw needn't show every extreme that they name: lengths[b] earlier tokens of request b are in the cache; the largest equals 2047 in every draw. The new token of request b goes to slot write_pos[b]; its earlier tokens fill the slots before it, going back cyclically.
All inputs are finite; a program needn't handle non-finite values.
Results may differ from the reference program's by a relative error of at most 0.0064.
Values may be sent and summed in bfloat16 or wider, within the bound.
A program may use at most 64 MiB of HBM per device.

```python
import math
import jax
import jax.numpy as jnp
from jax import lax

D = 4096
FF = 12288
H = 16
HD = 256
WINDOW = 2048
TOKENS = 32
N_REQ = 16
N_CH = 2


def draw_tokens(key, part):
    first_key = jax.random.fold_in(jax.random.fold_in(key, 11), 0)
    ramp = jnp.exp(math.log(3.0) * jnp.arange(D, dtype=jnp.float32) / D)
    base = jnp.clip(jax.random.normal(first_key, (TOKENS, D), jnp.float32), -6.0, 6.0)
    return (base * ramp[None, :]).astype(jnp.bfloat16)


def draw_cache(key, part):
    first_key = jax.random.fold_in(jax.random.fold_in(key, 23), 0)
    base = jnp.clip(jax.random.normal(first_key, (2, TOKENS, HD, WINDOW), jnp.float32), -6.0, 6.0)
    return base.astype(jnp.bfloat16)


def draw_lengths(key, part):
    first_key, second_key = jax.random.split(jax.random.fold_in(key, 37))
    uniform_int = jax.random.randint(first_key, (TOKENS,), 0, WINDOW, dtype=jnp.int32)
    cubed = uniform_int * uniform_int // WINDOW * uniform_int // WINDOW
    counts = 1 + cubed
    chosen = jax.random.randint(second_key, (), 0, TOKENS, dtype=jnp.int32)
    counts = jnp.where(jnp.arange(TOKENS, dtype=jnp.int32) == chosen, WINDOW - 1, counts)
    return counts.astype(jnp.int32)


def plant(values, key, least, high):
    longest = values.shape.index(max(values.shape))
    spots = []
    for shift in (0, 1):
        where = [jax.random.randint(jax.random.fold_in(key, axis), (), 0, length) for axis, length in enumerate(values.shape)]
        where[longest] = (where[longest] + shift) % values.shape[longest]
        spots.append(tuple(where))
    return values.at[spots[0]].set(least).at[spots[1]].set(high)


def steps_of(stream_key, extent, cuts, smallest, top_value):
    def one(dim, parts):
        draws = jax.random.uniform(jax.random.fold_in(jax.random.fold_in(stream_key, 6), dim), (parts,), jnp.float32, smallest / len(cuts), top_value / len(cuts))
        return jnp.repeat(jnp.exp(draws), extent[dim] // parts).reshape((-1,) + (1,) * (len(extent) - dim - 1))

    loudness = one(*cuts[0])
    for cut in cuts[1:]:
        loudness = loudness * one(*cut)
    return loudness


def gaussian(key, dims, width, most, cuts=(), kind=jnp.bfloat16):
    level = steps_of(key, dims, cuts, -0.22, 0.18) if cuts else 1.0
    array = jax.random.normal(key, dims, jnp.float32) * width * level
    return jnp.minimum(jnp.maximum(array, -most), most).astype(kind)


def setup_inputs(seed: int = 0) -> dict:
    arg_keys = jax.random.split(jax.random.key(seed), 12)
    return {
        "tokens": draw_tokens(jax.random.fold_in(arg_keys[11], 71), 0),
        "attn_gain": jnp.clip(1.0 + 0.18 * jax.random.normal(arg_keys[1], (D,), jnp.float32), 0.1, 1.9),
        "w_query": gaussian(arg_keys[2], (D, D), D ** -0.5, 0.09375, ((0, 2), (1, 16))),
        "w_keyval": gaussian(arg_keys[3], (D, 2 * HD), D ** -0.5, 0.09375, ((0, 2), (1, 16))),
        "cache": draw_cache(jax.random.fold_in(arg_keys[11], 71), 0),
        "lengths": draw_lengths(jax.random.fold_in(arg_keys[11], 71), 0),
        "write_pos": plant(jax.random.randint(arg_keys[6], (TOKENS,), 0, WINDOW), jax.random.fold_in(arg_keys[6], 1), 0, WINDOW - 1).astype(jnp.int32),
        "w_out": gaussian(arg_keys[7], (D, D), D ** -0.5, 0.09375, ((0, 2), (1, 16))),
        "mlp_gain": jnp.clip(1.0 + 0.18 * jax.random.normal(arg_keys[8], (D,), jnp.float32), 0.1, 1.9),
        "w_gate_up": gaussian(arg_keys[9], (D, 2 * FF), D ** -0.5, 0.09375, ((0, 2), (1, 16))),
        "w_down": gaussian(arg_keys[10], (FF, D), FF ** -0.5, 0.0546875, ((0, 16), (1, 2))),
    }


EPSILON = 1e-06

def rms_norm(values, gain):
    wide = values.astype(jnp.float32)
    meansq = lax.optimization_barrier(jnp.mean(wide * wide, axis=-1, keepdims=True))
    return (wide * lax.rsqrt(meansq + EPSILON) * gain).astype(jnp.bfloat16)

def attend_one(inputs):
    query, key_new, value_new, keys, values, length, position = inputs
    slots = jnp.arange(WINDOW, dtype=jnp.int32)
    offset = (position - 1 - slots) % WINDOW
    usable = offset < length
    factor = 1.0 / math.sqrt(HD)
    query_wide = query.astype(jnp.float32)
    scores = jnp.einsum('he,ew->hw', query_wide, keys.astype(jnp.float32)) * factor
    scores = jnp.where(usable[None, :], scores, -jnp.inf)
    own = lax.optimization_barrier(jnp.sum(query_wide * key_new.astype(jnp.float32)[None, :], axis=-1)) * factor
    top = jnp.maximum(lax.optimization_barrier(jnp.max(scores, axis=-1)), own)
    weights = jnp.exp(scores - top[:, None])
    own_weight = jnp.exp(own - top)
    total = lax.optimization_barrier(jnp.sum(weights, axis=-1)) + own_weight
    numer = jnp.einsum('hw,ew->he', weights.astype(jnp.bfloat16).astype(jnp.float32), values.astype(jnp.float32))
    numer = numer + own_weight.astype(jnp.bfloat16).astype(jnp.float32)[:, None] * value_new.astype(jnp.float32)[None, :]
    return (numer / total[:, None]).astype(jnp.bfloat16)

def reference(tokens, attn_gain, w_query, w_keyval, cache, lengths, write_pos, w_out, mlp_gain, w_gate_up, w_down):
    chan = HD // N_CH
    ffdev = FF // N_REQ
    normed = rms_norm(tokens, attn_gain)
    query = jnp.dot(normed, w_query, preferred_element_type=jnp.float32).astype(jnp.bfloat16)
    kv_new = jnp.dot(normed, w_keyval, preferred_element_type=jnp.float32).astype(jnp.bfloat16)
    heads_query = query.reshape(TOKENS, N_CH, H, chan).transpose(0, 2, 1, 3).reshape(TOKENS, H, HD)
    split_kv = kv_new.reshape(TOKENS, N_CH, 2, chan)
    key_new = split_kv[:, :, 0, :].reshape(TOKENS, HD)
    value_new = split_kv[:, :, 1, :].reshape(TOKENS, HD)
    mixed = lax.map(attend_one, (heads_query, key_new, value_new, cache[0], cache[1], lengths, write_pos))
    attn = mixed.reshape(TOKENS, H, N_CH, chan).transpose(0, 2, 1, 3).reshape(TOKENS, D)
    first = tokens.astype(jnp.float32) + jnp.dot(attn, w_out, preferred_element_type=jnp.float32)
    first = first.astype(jnp.bfloat16)
    normed_two = rms_norm(first, mlp_gain)
    joined = jnp.dot(normed_two, w_gate_up, preferred_element_type=jnp.float32).reshape(TOKENS, N_REQ, 2, ffdev)
    gate = joined[:, :, 0, :].reshape(TOKENS, FF)
    upward = joined[:, :, 1, :].reshape(TOKENS, FF)
    hidden = (jax.nn.gelu(gate, approximate=True) * upward).astype(jnp.bfloat16)
    result = first.astype(jnp.float32) + jnp.dot(hidden, w_down, preferred_element_type=jnp.float32)
    return (result.astype(jnp.bfloat16), kv_new)
```

```python
import math

import jax
import jax.numpy as jnp
from jax import lax
from jax.experimental import pallas as pl
from jax.experimental.pallas import tpu as pltpu
from jax.sharding import PartitionSpec as P

D = 4096
H = 16
HD = 256


EPSILON = 1e-06


def rms_norm(values, gain):
    wide = values.astype(jnp.float32)
    squares = jnp.sum(wide * wide, axis=1)
    summed = lax.psum(squares, "ch")
    meansq = summed / D
    return (wide * lax.rsqrt(meansq + EPSILON)[:, None] * gain[None, :]).astype(jnp.bfloat16)


def body(
    tokens,
    attn_gain,
    w_query,
    w_keyval,
    cache,
    lengths,
    write_pos,
    w_out,
    mlp_gain,
    w_gate_up,
    w_down,
):
    rows = tokens.shape[0]
    chan = cache.shape[2]
    window = cache.shape[3]
    factor = 1.0 / math.sqrt(HD)
    normed = rms_norm(tokens, attn_gain)
    joined = jnp.concatenate([w_query, w_keyval], axis=1)
    head_parts = jnp.dot(
        lax.all_gather(normed, "req", axis=0, tiled=True),
        joined,
        preferred_element_type=jnp.float32,
    )
    query_cols = w_query.shape[1]
    query_part, keyval_part = (
        lax.all_to_all(head_parts[:, :query_cols], "req", split_axis=0, concat_axis=1, tiled=True),
        lax.all_to_all(head_parts[:, query_cols:], "req", split_axis=0, concat_axis=1, tiled=True),
    )
    query_sum, keyval_sum = (
        lax.psum_scatter(query_part, "ch", scatter_dimension=1, tiled=True),
        lax.psum_scatter(keyval_part, "ch", scatter_dimension=1, tiled=True),
    )
    queries = query_sum.astype(jnp.bfloat16).reshape(rows, H, chan)
    keyval_new = keyval_sum.astype(jnp.bfloat16)
    key_new = keyval_new[:, :chan]
    value_new = keyval_new[:, chan:]
    keys = cache[0]
    values_cache = cache[1]
    own_part = jnp.sum(
        queries.astype(jnp.float32) * key_new.astype(jnp.float32)[:, None, :], axis=-1
    )
    score_part = jnp.einsum("bhe,bew->bhw", queries, keys, preferred_element_type=jnp.float32)
    summed, own_sum = lax.psum((score_part, own_part), "ch")
    slot_index = jnp.arange(window, dtype=jnp.int32)
    offset = (write_pos[:, None] - 1 - slot_index[None, :]) % window
    usable = offset < lengths[:, None]
    scores = jnp.where(usable[:, None, :], summed * factor, -jnp.inf)
    own_score = own_sum * factor
    top = jnp.maximum(jnp.max(scores, axis=-1), own_score)
    weights = jnp.exp(scores - top[..., None])
    own_weight = jnp.exp(own_score - top)
    total = jnp.sum(weights, axis=-1) + own_weight
    weights_low = weights.astype(jnp.bfloat16)
    numer = jnp.einsum(
        "bhw,bew->bhe", weights_low, values_cache, preferred_element_type=jnp.float32
    )
    numer = (
        numer
        + own_weight.astype(jnp.bfloat16).astype(jnp.float32)[..., None]
        * value_new.astype(jnp.float32)[:, None, :]
    )
    attn_local = (numer / total[..., None]).astype(jnp.bfloat16).reshape(rows, H * chan)
    out_parts = jnp.dot(
        lax.all_gather(attn_local, "req", axis=0, tiled=True),
        w_out,
        preferred_element_type=jnp.float32,
    )
    out_part = lax.all_to_all(out_parts, "req", split_axis=0, concat_axis=1, tiled=True)
    out_sum = lax.psum_scatter(out_part, "ch", scatter_dimension=1, tiled=True)
    first = (tokens.astype(jnp.float32) + out_sum).astype(jnp.bfloat16)
    normed_two = rms_norm(first, mlp_gain)
    hidden_cols = w_gate_up.shape[1] // 2
    ffn_parts = jnp.dot(
        lax.all_gather(normed_two, "req", axis=0, tiled=True),
        w_gate_up,
        preferred_element_type=jnp.float32,
    )
    ffn_total = lax.psum(ffn_parts, "ch")
    hidden = (
        jax.nn.gelu(ffn_total[:, :hidden_cols], approximate=True) * ffn_total[:, hidden_cols:]
    ).astype(jnp.bfloat16)
    down_sum = lax.psum_scatter(
        jnp.dot(hidden, w_down, preferred_element_type=jnp.float32),
        "req",
        scatter_dimension=0,
        tiled=True,
    )
    layer_out = (first.astype(jnp.float32) + down_sum).astype(jnp.bfloat16)
    return (layer_out, keyval_new)


REQ = 16
CH = 2
ROWS = 2
LANES = 128
CHUNKS = 16
HALF = REQ // CH
BLOCK = ROWS * CHUNKS
TILE = 8
MESH = pl.DeviceIdType.MESH


def place(chunk):
    return (chunk % 2) * HALF + chunk // 2


def fused_kernel(
    tokens_ref,
    attn_gain_ref,
    w_query_hbm,
    w_keyval_hbm,
    cache_hbm,
    lengths_ref,
    write_pos_ref,
    w_out_hbm,
    mlp_gain_ref,
    w_gate_up_hbm,
    w_down_hbm,
    out_ref,
    kv_ref,
    w_query,
    w_keyval,
    keys,
    values,
    w_out,
    w_gate_up,
    w_down,
    own_block,
    sends,
    gathered,
    wide,
    parts_out,
    parts_in,
    score_out,
    score_in,
    own_out,
    own_in,
    square_out,
    square_in,
    ffn_own,
    ffn_out,
    ffn_in,
    down_wide,
    down_out,
    down_in,
    result,
    load_sem,
    gather_send,
    gather_recv,
    parts_send,
    parts_recv,
    score_send,
    score_recv,
    own_send,
    own_recv,
    square_send,
    square_recv,
    ffn_send,
    ffn_recv,
    down_send,
    down_recv,
):
    req = lax.axis_index("req")
    ch = lax.axis_index("ch")
    other = 1 - ch
    window = keys.shape[2]
    hidden_cols = w_down.shape[0]
    factor = 1.0 / math.sqrt(HD)
    f32 = jnp.float32
    bf16 = jnp.bfloat16

    barrier = pltpu.get_barrier_semaphore()
    me = req * CH + ch

    def greet(step, carry):
        peer = (me + step) % (REQ * CH)
        pl.semaphore_signal(barrier, inc=1, device_id=(peer // CH, peer % CH), device_id_type=MESH)
        return carry

    lax.fori_loop(1, REQ * CH, greet, 0)

    loads = [
        pltpu.make_async_copy(src, dst, load_sem.at[index])
        for index, (src, dst) in enumerate(
            (
                (w_query_hbm, w_query),
                (w_keyval_hbm, w_keyval),
                (cache_hbm.at[0], keys),
                (cache_hbm.at[1], values),
                (w_out_hbm, w_out),
                (w_gate_up_hbm, w_gate_up),
                (w_down_hbm, w_down),
            )
        )
    ]
    for load in loads:
        load.start()

    tokens = tokens_ref[...].astype(f32)
    for row in range(ROWS):
        for chunk in range(CHUNKS):
            spot = row * CHUNKS + place(chunk)
            own_block[spot : spot + 1, :] = tokens[row : row + 1, chunk * LANES : (chunk + 1) * LANES]

    pl.semaphore_wait(barrier, REQ * CH - 1)

    def block_of(index):
        return pl.ds(pl.multiple_of(index * BLOCK, BLOCK), BLOCK)

    def tile_of(index):
        return pl.ds(pl.multiple_of(index * TILE, TILE), TILE)

    def gather_copy(phase, peer, slot):
        return pltpu.make_async_remote_copy(
            src_ref=sends.at[phase],
            dst_ref=gathered.at[phase, block_of(slot)],
            send_sem=gather_send.at[phase, peer],
            recv_sem=gather_recv.at[phase, slot],
            device_id=(peer, ch),
            device_id_type=MESH,
        )

    def gather(phase, block):
        sends[phase] = block
        gathered[phase, block_of(req), :] = block

        def start(step, carry):
            peer = (req + step) % REQ
            gather_copy(phase, peer, req).start()
            return carry

        lax.fori_loop(1, REQ, start, 0)

    def gather_wait(phase):
        def wait(step, carry):
            peer = (req + REQ - step) % REQ
            gather_copy(phase, peer, peer).wait_recv()
            return carry

        lax.fori_loop(1, REQ, wait, 0)
        wide[phase] = gathered[phase].astype(f32)

    def chunk_rows(phase, chunk):
        spot = place(chunk)
        return jnp.concatenate(
            [wide[phase, pl.ds(row * CHUNKS + spot, REQ, stride=BLOCK), :] for row in range(ROWS)],
            axis=0,
        )

    def gained(phase, gain_ref):
        total = None
        pieces = []
        for chunk in range(CHUNKS):
            piece = chunk_rows(phase, chunk)
            square = piece * piece
            total = square if total is None else total + square
            pieces.append((piece * gain_ref[:, chunk * LANES : (chunk + 1) * LANES]).astype(bf16))
        return jnp.concatenate(pieces, axis=1), jnp.sum(total, axis=1, keepdims=True)

    def parts_copy(phase, peer, slot):
        return pltpu.make_async_remote_copy(
            src_ref=parts_out.at[phase, tile_of(peer)],
            dst_ref=parts_in.at[phase, tile_of(slot)],
            send_sem=parts_send.at[phase, peer],
            recv_sem=parts_recv.at[phase, slot],
            device_id=(peer, req // HALF),
            device_id_type=MESH,
        )

    my_slot = ch * HALF + req % HALF

    def is_self(peer):
        return jnp.logical_and(peer == req, req // HALF == ch)

    def scatter(phase, rows):
        for index, piece in enumerate(rows):
            parts_out[phase, pl.ds(index, REQ, stride=TILE), :] = piece

        def start(step, carry):
            peer = (req + step) % REQ

            @pl.when(jnp.logical_not(is_self(peer)))
            def _():
                parts_copy(phase, peer, my_slot).start()

            return carry

        lax.fori_loop(0, REQ, start, 0)

        @pl.when(req // HALF == ch)
        def _():
            parts_in[phase, tile_of(my_slot), :] = parts_out[phase, tile_of(req), :]

    def scatter_wait(phase):
        def wait(slot, carry):
            mine = jnp.logical_and(slot == my_slot, req // HALF == ch)

            @pl.when(jnp.logical_not(mine))
            def _():
                parts_copy(phase, req, slot).wait_recv()

            return carry

        lax.fori_loop(0, CH * HALF, wait, 0)

    def summed(phase, index):
        pieces = parts_in[phase, pl.ds(index, CH * HALF, stride=TILE), :]
        return pieces[:HALF] + pieces[HALF:]

    gather(0, own_block[...].astype(bf16))
    loads[0].wait()
    loads[1].wait()
    gather_wait(0)
    lhs, squares = gained(0, attn_gain_ref)
    query_part = jnp.dot(lhs, w_query[...], preferred_element_type=f32)
    keyval_part = jnp.dot(lhs, w_keyval[...], preferred_element_type=f32)
    per_row = LANES // keyval_part.shape[1]
    lane = lax.broadcasted_iota(jnp.int32, (ROWS * REQ, LANES), 1)
    keyval_part = jnp.where(
        lane // keyval_part.shape[1] == req % per_row,
        jnp.concatenate([keyval_part] * per_row, axis=1),
        0.0,
    )
    squares = jnp.broadcast_to(squares, (ROWS * REQ, LANES))

    def by_row(array):
        return [array[row * REQ : (row + 1) * REQ] for row in range(ROWS)]

    scatter(
        0,
        by_row(query_part[:, :LANES])
        + by_row(query_part[:, LANES:])
        + by_row(keyval_part)
        + by_row(squares),
    )
    loads[2].wait()
    scatter_wait(0)

    def score_copy(row):
        return pltpu.make_async_remote_copy(
            src_ref=score_out.at[row],
            dst_ref=score_in.at[row],
            send_sem=score_send.at[row],
            recv_sem=score_recv.at[row],
            device_id=(req, other),
            device_id_type=MESH,
        )

    own_copy = pltpu.make_async_remote_copy(
        src_ref=own_out,
        dst_ref=own_in,
        send_sem=own_send.at[0],
        recv_sem=own_recv.at[0],
        device_id=(req, other),
        device_id_type=MESH,
    )
    values_new = []
    for row in range(ROWS):
        scale = lax.rsqrt(summed(0, 6 + row)[:1, :] / D + EPSILON)
        query = (jnp.concatenate([summed(0, row), summed(0, 2 + row)], axis=0) * scale).astype(bf16)
        score_out[row] = jnp.dot(query, keys[row], preferred_element_type=f32)
        score_copy(row).start()
        keyval = summed(0, 4 + row) * scale
        key_new = jnp.sum(keyval[: HALF // 2], axis=0, keepdims=True).astype(bf16)
        value_new = jnp.sum(keyval[HALF // 2 :], axis=0, keepdims=True).astype(bf16)
        own = jnp.sum(query.astype(f32) * key_new.astype(f32), axis=1, keepdims=True)
        own_out[row] = jnp.broadcast_to(own, (H, LANES))
        values_new.append(value_new.astype(f32))
        result[row : row + 1, :LANES] = key_new.astype(f32)
        result[row : row + 1, LANES : 2 * LANES] = value_new.astype(f32)
    own_copy.start()
    kv_ref[...] = result[:, : 2 * LANES].astype(bf16)
    loads[3].wait()
    mixed = []
    slot_index = lax.broadcasted_iota(jnp.int32, (H, window), 1)
    for row in range(ROWS):
        score_copy(row).wait_recv()
        if row == 0:
            own_copy.wait_recv()
        offset = write_pos_ref[row] - 1 - slot_index
        offset = jnp.where(offset < 0, offset + window, offset)
        scores = jnp.where(
            offset < lengths_ref[row], (score_out[row] + score_in[row]) * factor, -jnp.inf
        )
        own = (own_out[row] + own_in[row])[:, :1] * factor
        top = jnp.maximum(jnp.max(scores, axis=1, keepdims=True), own)
        weights = jnp.exp(scores - top)
        own_weight = jnp.exp(own - top)
        total = jnp.sum(weights, axis=1, keepdims=True) + own_weight
        numer = lax.dot_general(
            weights.astype(bf16), values[row], (((1,), (1,)), ((), ())), preferred_element_type=f32
        )
        numer = numer + own_weight.astype(bf16).astype(f32) * values_new[row]
        mixed.append(numer / total)

    gather(1, jnp.concatenate(mixed, axis=0).astype(bf16))
    loads[4].wait()
    gather_wait(1)
    lhs = jnp.concatenate([chunk_rows(1, chunk) for chunk in range(CHUNKS)], axis=1).astype(bf16)
    out_part = jnp.dot(lhs, w_out[...], preferred_element_type=f32)
    scatter(1, by_row(out_part[:, :LANES]) + by_row(out_part[:, LANES:]))
    scatter_wait(1)
    first = jnp.concatenate(
        [piece for row in range(ROWS) for piece in (summed(1, row), summed(1, 2 + row))], axis=0
    )
    first = (own_block[...] + first).astype(bf16)
    own_block[...] = first.astype(f32)

    gather(2, first)
    loads[5].wait()
    loads[6].wait()
    gather_wait(2)
    lhs, squares = gained(2, mlp_gain_ref)
    square_out[...] = jnp.broadcast_to(squares, (ROWS * REQ, LANES))
    square_copy = pltpu.make_async_remote_copy(
        src_ref=square_out,
        dst_ref=square_in,
        send_sem=square_send.at[0],
        recv_sem=square_recv.at[0],
        device_id=(req, other),
        device_id_type=MESH,
    )
    square_copy.start()
    pieces, _, double = ffn_own.shape
    width = double // 2

    def ffn_copy(piece):
        return pltpu.make_async_remote_copy(
            src_ref=ffn_out.at[piece],
            dst_ref=ffn_in.at[piece],
            send_sem=ffn_send.at[piece],
            recv_sem=ffn_recv.at[piece],
            device_id=(req, other),
            device_id_type=MESH,
        )

    for piece in range(pieces):
        for part in range(2):
            begin = part * hidden_cols + piece * width
            block = jnp.dot(lhs, w_gate_up[:, begin : begin + width], preferred_element_type=f32)
            ffn_own[piece, :, part * width : (part + 1) * width] = block
            ffn_out[piece, :, part * width : (part + 1) * width] = block.astype(bf16)
        ffn_copy(piece).start()
    square_copy.wait_recv()
    scale = lax.rsqrt((square_out[...] + square_in[...])[:, :1] / D + EPSILON)
    hidden = []
    for piece in range(pieces):
        ffn_copy(piece).wait_recv()
        both = (ffn_own[piece] + ffn_in[piece].astype(f32)) * scale
        hidden.append(
            (jax.nn.gelu(both[:, :width], approximate=True) * both[:, width:]).astype(bf16)
        )
    hidden = jnp.concatenate(hidden, axis=1)

    down = jnp.dot(hidden, w_down[...], preferred_element_type=f32)
    for chunk in range(CHUNKS):
        columns = down[:, chunk * LANES : (chunk + 1) * LANES]
        for row in range(ROWS):
            down_wide[pl.ds(row * CHUNKS + place(chunk), REQ, stride=BLOCK), :] = columns[
                row * REQ : (row + 1) * REQ
            ]
    down_out[...] = down_wide[...].astype(bf16)

    def down_copy(peer, slot):
        return pltpu.make_async_remote_copy(
            src_ref=down_out.at[block_of(peer)],
            dst_ref=down_in.at[block_of(slot)],
            send_sem=down_send.at[peer],
            recv_sem=down_recv.at[slot],
            device_id=(peer, ch),
            device_id_type=MESH,
        )

    def down_start(step, carry):
        peer = (req + step) % REQ
        down_copy(peer, req).start()
        return carry

    lax.fori_loop(1, REQ, down_start, 0)
    down_in[block_of(req), :] = down_out[block_of(req), :]

    def down_wait(step, carry):
        peer = (req + REQ - step) % REQ
        down_copy(peer, peer).wait_recv()
        return carry

    lax.fori_loop(1, REQ, down_wait, 0)
    total = down_in[:BLOCK, :].astype(f32)
    for index in range(1, REQ):
        total = total + down_in[index * BLOCK : (index + 1) * BLOCK, :].astype(f32)
    total = total + own_block[...]
    for row in range(ROWS):
        for chunk in range(CHUNKS):
            spot = row * CHUNKS + place(chunk)
            result[row : row + 1, chunk * LANES : (chunk + 1) * LANES] = total[spot : spot + 1]
    out_ref[...] = result[...].astype(bf16)

    def drain(step, carry):
        peer = (req + step) % REQ
        for phase in range(3):
            gather_copy(phase, peer, req).wait_send()
        down_copy(peer, req).wait_send()
        return carry

    lax.fori_loop(1, REQ, drain, 0)

    def drain_parts(peer, carry):
        @pl.when(jnp.logical_not(is_self(peer)))
        def _():
            for phase in range(2):
                parts_copy(phase, peer, my_slot).wait_send()

        return carry

    lax.fori_loop(0, REQ, drain_parts, 0)
    for row in range(ROWS):
        score_copy(row).wait_send()
    own_copy.wait_send()
    square_copy.wait_send()
    for piece in range(pieces):
        ffn_copy(piece).wait_send()


def fused(
    tokens,
    attn_gain,
    w_query,
    w_keyval,
    cache,
    lengths,
    write_pos,
    w_out,
    mlp_gain,
    w_gate_up,
    w_down,
):
    f32 = jnp.float32
    bf16 = jnp.bfloat16
    window = cache.shape[3]
    pieces = w_down.shape[0] // 256
    every = ROWS * REQ
    vmem = pl.BlockSpec(memory_space=pltpu.VMEM)
    smem = pl.BlockSpec(memory_space=pltpu.SMEM)
    hbm = pl.BlockSpec(memory_space=pl.ANY)
    dma = pltpu.SemaphoreType.DMA
    return pl.pallas_call(
        fused_kernel,
        out_shape=(
            jax.ShapeDtypeStruct(tokens.shape, bf16),
            jax.ShapeDtypeStruct((ROWS, 2 * LANES), bf16),
        ),
        in_specs=[vmem, vmem, hbm, hbm, hbm, smem, smem, hbm, vmem, hbm, hbm],
        out_specs=(vmem, vmem),
        scratch_shapes=[
            pltpu.VMEM(w_query.shape, bf16),
            pltpu.VMEM(w_keyval.shape, bf16),
            pltpu.VMEM(cache.shape[1:], bf16),
            pltpu.VMEM(cache.shape[1:], bf16),
            pltpu.VMEM(w_out.shape, bf16),
            pltpu.VMEM(w_gate_up.shape, bf16),
            pltpu.VMEM(w_down.shape, bf16),
            pltpu.VMEM((BLOCK, LANES), f32),
            pltpu.VMEM((3, BLOCK, LANES), bf16),
            pltpu.VMEM((3, REQ * BLOCK, LANES), bf16),
            pltpu.VMEM((3, REQ * BLOCK, LANES), f32),
            pltpu.VMEM((2, REQ * TILE, LANES), f32),
            pltpu.VMEM((2, CH * HALF * TILE, LANES), f32),
            pltpu.VMEM((ROWS, H, window), f32),
            pltpu.VMEM((ROWS, H, window), f32),
            pltpu.VMEM((ROWS, H, LANES), f32),
            pltpu.VMEM((ROWS, H, LANES), f32),
            pltpu.VMEM((every, LANES), f32),
            pltpu.VMEM((every, LANES), f32),
            pltpu.VMEM((pieces, every, 512), f32),
            pltpu.VMEM((pieces, every, 512), bf16),
            pltpu.VMEM((pieces, every, 512), bf16),
            pltpu.VMEM((REQ * BLOCK, LANES), f32),
            pltpu.VMEM((REQ * BLOCK, LANES), bf16),
            pltpu.VMEM((REQ * BLOCK, LANES), bf16),
            pltpu.VMEM(tokens.shape, f32),
            dma((7,)),
            dma((3, REQ)),
            dma((3, REQ)),
            dma((2, REQ)),
            dma((2, CH * HALF)),
            dma((ROWS,)),
            dma((ROWS,)),
            dma((1,)),
            dma((1,)),
            dma((1,)),
            dma((1,)),
            dma((pieces,)),
            dma((pieces,)),
            dma((REQ,)),
            dma((REQ,)),
        ],
        compiler_params=pltpu.CompilerParams(
            collective_id=0, has_side_effects=True, vmem_limit_bytes=48 * 1024 * 1024
        ),
    )(
        tokens,
        attn_gain.reshape(1, -1),
        w_query,
        w_keyval,
        cache,
        lengths,
        write_pos,
        w_out,
        mlp_gain.reshape(1, -1),
        w_gate_up,
        w_down,
    )


def solution(mesh):
    placed = (
        P("req", "ch"),
        P("ch"),
        P("ch", "req"),
        P("ch", "req"),
        P(None, "req", "ch", None),
        P("req"),
        P("req"),
        P("ch", "req"),
        P("ch"),
        P("ch", "req"),
        P("req", "ch"),
    )
    def step(*args):
        tokens, cache = args[0], args[4]
        fits = (
            mesh.shape["ch"] == CH
            and mesh.shape["req"] == REQ
            and tokens.shape[0] == ROWS
            and tokens.shape[1] == CHUNKS * LANES
            and cache.shape[2] == LANES
        )
        return (fused if fits else body)(*args)

    return jax.shard_map(
        step,
        mesh=mesh,
        in_specs=placed,
        out_specs=(P("req", "ch"), P("req", "ch")),
        check_vma=False,
    )
```

```python
import math

import jax
import jax.numpy as jnp
from jax import lax
from jax.experimental import pallas as pl
from jax.experimental.pallas import tpu as pltpu
from jax.sharding import PartitionSpec as P

D = 4096
H = 16
HD = 256


EPSILON = 1e-06


def rms_norm(values, gain):
    wide = values.astype(jnp.float32)
    squares = jnp.sum(wide * wide, axis=1)
    summed = lax.psum(squares, "ch")
    meansq = summed / D
    return (wide * lax.rsqrt(meansq + EPSILON)[:, None] * gain[None, :]).astype(jnp.bfloat16)


def body(
    tokens,
    attn_gain,
    w_query,
    w_keyval,
    cache,
    lengths,
    write_pos,
    w_out,
    mlp_gain,
    w_gate_up,
    w_down,
):
    rows = tokens.shape[0]
    chan = cache.shape[2]
    window = cache.shape[3]
    factor = 1.0 / math.sqrt(HD)
    normed = rms_norm(tokens, attn_gain)
    joined = jnp.concatenate([w_query, w_keyval], axis=1)
    head_parts = jnp.dot(
        lax.all_gather(normed, "req", axis=0, tiled=True),
        joined,
        preferred_element_type=jnp.float32,
    )
    query_cols = w_query.shape[1]
    query_part, keyval_part = (
        lax.all_to_all(head_parts[:, :query_cols], "req", split_axis=0, concat_axis=1, tiled=True),
        lax.all_to_all(head_parts[:, query_cols:], "req", split_axis=0, concat_axis=1, tiled=True),
    )
    query_sum, keyval_sum = (
        lax.psum_scatter(query_part, "ch", scatter_dimension=1, tiled=True),
        lax.psum_scatter(keyval_part, "ch", scatter_dimension=1, tiled=True),
    )
    queries = query_sum.astype(jnp.bfloat16).reshape(rows, H, chan)
    keyval_new = keyval_sum.astype(jnp.bfloat16)
    key_new = keyval_new[:, :chan]
    value_new = keyval_new[:, chan:]
    keys = cache[0]
    values_cache = cache[1]
    own_part = jnp.sum(
        queries.astype(jnp.float32) * key_new.astype(jnp.float32)[:, None, :], axis=-1
    )
    score_part = jnp.einsum("bhe,bew->bhw", queries, keys, preferred_element_type=jnp.float32)
    summed, own_sum = lax.psum((score_part, own_part), "ch")
    slot_index = jnp.arange(window, dtype=jnp.int32)
    offset = (write_pos[:, None] - 1 - slot_index[None, :]) % window
    usable = offset < lengths[:, None]
    scores = jnp.where(usable[:, None, :], summed * factor, -jnp.inf)
    own_score = own_sum * factor
    top = jnp.maximum(jnp.max(scores, axis=-1), own_score)
    weights = jnp.exp(scores - top[..., None])
    own_weight = jnp.exp(own_score - top)
    total = jnp.sum(weights, axis=-1) + own_weight
    weights_low = weights.astype(jnp.bfloat16)
    numer = jnp.einsum(
        "bhw,bew->bhe", weights_low, values_cache, preferred_element_type=jnp.float32
    )
    numer = (
        numer
        + own_weight.astype(jnp.bfloat16).astype(jnp.float32)[..., None]
        * value_new.astype(jnp.float32)[:, None, :]
    )
    attn_local = (numer / total[..., None]).astype(jnp.bfloat16).reshape(rows, H * chan)
    out_parts = jnp.dot(
        lax.all_gather(attn_local, "req", axis=0, tiled=True),
        w_out,
        preferred_element_type=jnp.float32,
    )
    out_part = lax.all_to_all(out_parts, "req", split_axis=0, concat_axis=1, tiled=True)
    out_sum = lax.psum_scatter(out_part, "ch", scatter_dimension=1, tiled=True)
    first = (tokens.astype(jnp.float32) + out_sum).astype(jnp.bfloat16)
    normed_two = rms_norm(first, mlp_gain)
    hidden_cols = w_gate_up.shape[1] // 2
    ffn_parts = jnp.dot(
        lax.all_gather(normed_two, "req", axis=0, tiled=True),
        w_gate_up,
        preferred_element_type=jnp.float32,
    )
    ffn_total = lax.psum(ffn_parts, "ch")
    hidden = (
        jax.nn.gelu(ffn_total[:, :hidden_cols], approximate=True) * ffn_total[:, hidden_cols:]
    ).astype(jnp.bfloat16)
    down_sum = lax.psum_scatter(
        jnp.dot(hidden, w_down, preferred_element_type=jnp.float32),
        "req",
        scatter_dimension=0,
        tiled=True,
    )
    layer_out = (first.astype(jnp.float32) + down_sum).astype(jnp.bfloat16)
    return (layer_out, keyval_new)


REQ = 16
CH = 2
ROWS = 2
LANES = 128
CHUNKS = 16
HALF = REQ // CH
BLOCK = ROWS * CHUNKS
TILE = 8
MESH = pl.DeviceIdType.MESH


def place(chunk):
    return (chunk % 2) * HALF + chunk // 2


def fused_kernel(
    tokens_hbm,
    attn_gain_hbm,
    w_query_hbm,
    w_keyval_hbm,
    cache_hbm,
    lengths_hbm,
    write_pos_hbm,
    w_out_hbm,
    mlp_gain_hbm,
    w_gate_up_hbm,
    w_down_hbm,
    out_ref,
    kv_ref,
    tokens_ref,
    attn_gain_ref,
    lengths_ref,
    write_pos_ref,
    mlp_gain_ref,
    w_query,
    w_keyval,
    keys,
    values,
    w_out,
    w_gate_up,
    w_down,
    own_block,
    sends,
    gathered,
    wide,
    parts_out,
    parts_in,
    score_out,
    score_in,
    own_out,
    own_in,
    square_out,
    square_in,
    ffn_own,
    ffn_out,
    ffn_in,
    down_wide,
    down_out,
    down_in,
    result,
    load_sem,
    gather_send,
    gather_recv,
    parts_send,
    parts_recv,
    score_send,
    score_recv,
    own_send,
    own_recv,
    square_send,
    square_recv,
    ffn_send,
    ffn_recv,
    down_send,
    down_recv,
):
    req = lax.axis_index("req")
    ch = lax.axis_index("ch")
    other = 1 - ch
    window = keys.shape[2]
    hidden_cols = w_down.shape[0]
    factor = 1.0 / math.sqrt(HD)
    f32 = jnp.float32
    bf16 = jnp.bfloat16

    drains = []

    def finish():
        for drain in drains:
            drain()

    barrier = pltpu.get_barrier_semaphore()
    me = req * CH + ch

    def greet(step, carry):
        peer = (me + step) % (REQ * CH)
        pl.semaphore_signal(barrier, inc=1, device_id=(peer // CH, peer % CH), device_id_type=MESH)
        return carry

    lax.fori_loop(1, REQ * CH, greet, 0)

    loads = [
        pltpu.make_async_copy(src, dst, load_sem.at[index])
        for index, (src, dst) in enumerate(
            (
                (tokens_hbm, tokens_ref),
                (attn_gain_hbm, attn_gain_ref),
                (w_query_hbm, w_query),
                (w_keyval_hbm, w_keyval),
                (lengths_hbm, lengths_ref),
                (write_pos_hbm, write_pos_ref),
                (cache_hbm.at[0], keys),
                (cache_hbm.at[1], values),
                (w_out_hbm, w_out),
                (mlp_gain_hbm, mlp_gain_ref),
                (w_gate_up_hbm, w_gate_up),
                (w_down_hbm, w_down),
            )
        )
    ]
    for load in loads:
        load.start()

    loads[0].wait()
    tokens = tokens_ref[...].astype(f32)
    for row in range(ROWS):
        for chunk in range(CHUNKS):
            spot = row * CHUNKS + place(chunk)
            own_block[spot : spot + 1, :] = tokens[row : row + 1, chunk * LANES : (chunk + 1) * LANES]

    pl.semaphore_wait(barrier, REQ * CH - 1)

    def block_of(index):
        return pl.ds(pl.multiple_of(index * BLOCK, BLOCK), BLOCK)

    def tile_of(index):
        return pl.ds(pl.multiple_of(index * TILE, TILE), TILE)

    def gather_copy(phase, peer, slot):
        return pltpu.make_async_remote_copy(
            src_ref=sends.at[phase],
            dst_ref=gathered.at[phase, block_of(slot)],
            send_sem=gather_send.at[phase, peer],
            recv_sem=gather_recv.at[phase, slot],
            device_id=(peer, ch),
            device_id_type=MESH,
        )

    def gather(phase, block):
        sends[phase] = block
        gathered[phase, block_of(req), :] = block

        def start(step, carry):
            peer = (req + step) % REQ
            gather_copy(phase, peer, req).start()
            return carry

        lax.fori_loop(1, REQ, start, 0)

        def drain(step, carry):
            gather_copy(phase, (req + step) % REQ, req).wait_send()
            return carry

        drains.append(lambda: lax.fori_loop(1, REQ, drain, 0))

    def gather_wait(phase):
        def wait(step, carry):
            peer = (req + REQ - step) % REQ
            gather_copy(phase, peer, peer).wait_recv()
            return carry

        lax.fori_loop(1, REQ, wait, 0)
        wide[phase] = gathered[phase].astype(f32)

    def chunk_rows(phase, chunk):
        spot = place(chunk)
        return jnp.concatenate(
            [wide[phase, pl.ds(row * CHUNKS + spot, REQ, stride=BLOCK), :] for row in range(ROWS)],
            axis=0,
        )

    def gained(phase, gain_ref):
        total = None
        pieces = []
        for chunk in range(CHUNKS):
            piece = chunk_rows(phase, chunk)
            square = piece * piece
            total = square if total is None else total + square
            pieces.append((piece * gain_ref[:, chunk * LANES : (chunk + 1) * LANES]).astype(bf16))
        return jnp.concatenate(pieces, axis=1), jnp.sum(total, axis=1, keepdims=True)

    def parts_copy(phase, peer, slot):
        return pltpu.make_async_remote_copy(
            src_ref=parts_out.at[phase, tile_of(peer)],
            dst_ref=parts_in.at[phase, tile_of(slot)],
            send_sem=parts_send.at[phase, peer],
            recv_sem=parts_recv.at[phase, slot],
            device_id=(peer, req // HALF),
            device_id_type=MESH,
        )

    my_slot = ch * HALF + req % HALF

    def is_self(peer):
        return jnp.logical_and(peer == req, req // HALF == ch)

    def scatter(phase, rows):
        for index, piece in enumerate(rows):
            parts_out[phase, pl.ds(index, REQ, stride=TILE), :] = piece

        def start(step, carry):
            peer = (req + step) % REQ

            @pl.when(jnp.logical_not(is_self(peer)))
            def _():
                parts_copy(phase, peer, my_slot).start()

            return carry

        lax.fori_loop(0, REQ, start, 0)

        def drain(peer, carry):
            @pl.when(jnp.logical_not(is_self(peer)))
            def _():
                parts_copy(phase, peer, my_slot).wait_send()

            return carry

        drains.append(lambda: lax.fori_loop(0, REQ, drain, 0))

        @pl.when(req // HALF == ch)
        def _():
            parts_in[phase, tile_of(my_slot), :] = parts_out[phase, tile_of(req), :]

    def scatter_wait(phase):
        def wait(slot, carry):
            mine = jnp.logical_and(slot == my_slot, req // HALF == ch)

            @pl.when(jnp.logical_not(mine))
            def _():
                parts_copy(phase, req, slot).wait_recv()

            return carry

        lax.fori_loop(0, CH * HALF, wait, 0)

    def summed(phase, index):
        pieces = parts_in[phase, pl.ds(index, CH * HALF, stride=TILE), :]
        return pieces[:HALF] + pieces[HALF:]

    gather(0, own_block[...].astype(bf16))
    for load in loads[1:4]:
        load.wait()
    gather_wait(0)
    lhs, squares = gained(0, attn_gain_ref)
    query_part = jnp.dot(lhs, w_query[...], preferred_element_type=f32)
    keyval_part = lax.dot_general(
        lhs, w_keyval[...], (((1,), (1,)), ((), ())), preferred_element_type=f32
    )
    per_row = LANES // keyval_part.shape[1]
    lane = lax.broadcasted_iota(jnp.int32, (ROWS * REQ, LANES), 1)
    keyval_part = jnp.where(
        lane // keyval_part.shape[1] == req % per_row,
        jnp.concatenate([keyval_part] * per_row, axis=1),
        0.0,
    )
    squares = jnp.broadcast_to(squares, (ROWS * REQ, LANES))

    def by_row(array):
        return [array[row * REQ : (row + 1) * REQ] for row in range(ROWS)]

    scatter(
        0,
        by_row(query_part[:, :LANES])
        + by_row(query_part[:, LANES:])
        + by_row(keyval_part)
        + by_row(squares),
    )
    for load in loads[4:7]:
        load.wait()
    scatter_wait(0)

    def score_copy(row):
        return pltpu.make_async_remote_copy(
            src_ref=score_out.at[row],
            dst_ref=score_in.at[row],
            send_sem=score_send.at[row],
            recv_sem=score_recv.at[row],
            device_id=(req, other),
            device_id_type=MESH,
        )

    own_copy = pltpu.make_async_remote_copy(
        src_ref=own_out,
        dst_ref=own_in,
        send_sem=own_send.at[0],
        recv_sem=own_recv.at[0],
        device_id=(req, other),
        device_id_type=MESH,
    )
    values_new = []
    for row in range(ROWS):
        scale = lax.rsqrt(summed(0, 6 + row)[:1, :] / D + EPSILON)
        query = (jnp.concatenate([summed(0, row), summed(0, 2 + row)], axis=0) * scale).astype(bf16)
        score_out[row] = jnp.dot(query, keys[row], preferred_element_type=f32)
        score_copy(row).start()
        drains.append(score_copy(row).wait_send)
        keyval = summed(0, 4 + row) * scale
        key_new = jnp.sum(keyval[: HALF // 2], axis=0, keepdims=True).astype(bf16)
        value_new = jnp.sum(keyval[HALF // 2 :], axis=0, keepdims=True).astype(bf16)
        own = jnp.sum(query.astype(f32) * key_new.astype(f32), axis=1, keepdims=True)
        own_out[row] = jnp.broadcast_to(own, (H, LANES))
        values_new.append(value_new.astype(f32))
        result[row : row + 1, :LANES] = key_new.astype(f32)
        result[row : row + 1, LANES : 2 * LANES] = value_new.astype(f32)
    own_copy.start()
    drains.append(own_copy.wait_send)
    kv_ref[...] = result[:, : 2 * LANES].astype(bf16)
    loads[7].wait()
    mixed = []
    slot_index = lax.broadcasted_iota(jnp.int32, (H, window), 1)
    for row in range(ROWS):
        score_copy(row).wait_recv()
        if row == 0:
            own_copy.wait_recv()
        offset = write_pos_ref[row] - 1 - slot_index
        offset = jnp.where(offset < 0, offset + window, offset)
        scores = jnp.where(
            offset < lengths_ref[row], (score_out[row] + score_in[row]) * factor, -jnp.inf
        )
        own = (own_out[row] + own_in[row])[:, :1] * factor
        top = jnp.maximum(jnp.max(scores, axis=1, keepdims=True), own)
        weights = jnp.exp(scores - top)
        own_weight = jnp.exp(own - top)
        total = jnp.sum(weights, axis=1, keepdims=True) + own_weight
        numer = lax.dot_general(
            weights.astype(bf16), values[row], (((1,), (1,)), ((), ())), preferred_element_type=f32
        )
        numer = numer + own_weight.astype(bf16).astype(f32) * values_new[row]
        mixed.append(numer / total)

    gather(1, jnp.concatenate(mixed, axis=0).astype(bf16))
    loads[8].wait()
    gather_wait(1)
    lhs = jnp.concatenate([chunk_rows(1, chunk) for chunk in range(CHUNKS)], axis=1).astype(bf16)
    out_part = jnp.dot(lhs, w_out[...], preferred_element_type=f32)
    scatter(1, by_row(out_part[:, :LANES]) + by_row(out_part[:, LANES:]))
    scatter_wait(1)
    first = jnp.concatenate(
        [piece for row in range(ROWS) for piece in (summed(1, row), summed(1, 2 + row))], axis=0
    )
    first = (own_block[...] + first).astype(bf16)
    own_block[...] = first.astype(f32)

    gather(2, first)
    for load in loads[9:]:
        load.wait()
    gather_wait(2)
    lhs, squares = gained(2, mlp_gain_ref)
    square_out[...] = jnp.broadcast_to(squares, (ROWS * REQ, LANES))
    square_copy = pltpu.make_async_remote_copy(
        src_ref=square_out,
        dst_ref=square_in,
        send_sem=square_send.at[0],
        recv_sem=square_recv.at[0],
        device_id=(req, other),
        device_id_type=MESH,
    )
    square_copy.start()
    drains.append(square_copy.wait_send)
    pieces, _, double = ffn_own.shape
    width = double // 2

    def ffn_copy(piece):
        return pltpu.make_async_remote_copy(
            src_ref=ffn_out.at[piece],
            dst_ref=ffn_in.at[piece],
            send_sem=ffn_send.at[piece],
            recv_sem=ffn_recv.at[piece],
            device_id=(req, other),
            device_id_type=MESH,
        )

    for piece in range(pieces):
        for part in range(2):
            begin = part * hidden_cols + piece * width
            block = jnp.dot(lhs, w_gate_up[:, begin : begin + width], preferred_element_type=f32)
            ffn_own[piece, :, part * width : (part + 1) * width] = block
            ffn_out[piece, :, part * width : (part + 1) * width] = block.astype(bf16)
        ffn_copy(piece).start()
        drains.append(ffn_copy(piece).wait_send)
    square_copy.wait_recv()
    scale = lax.rsqrt((square_out[...] + square_in[...])[:, :1] / D + EPSILON)
    hidden = []
    for piece in range(pieces):
        ffn_copy(piece).wait_recv()
        both = (ffn_own[piece] + ffn_in[piece].astype(f32)) * scale
        hidden.append(
            (jax.nn.gelu(both[:, :width], approximate=True) * both[:, width:]).astype(bf16)
        )
    hidden = jnp.concatenate(hidden, axis=1)

    down = jnp.dot(hidden, w_down[...], preferred_element_type=f32)
    for chunk in range(CHUNKS):
        columns = down[:, chunk * LANES : (chunk + 1) * LANES]
        for row in range(ROWS):
            down_wide[pl.ds(row * CHUNKS + place(chunk), REQ, stride=BLOCK), :] = columns[
                row * REQ : (row + 1) * REQ
            ]
    down_out[...] = down_wide[...].astype(bf16)

    def down_copy(peer, slot):
        return pltpu.make_async_remote_copy(
            src_ref=down_out.at[block_of(peer)],
            dst_ref=down_in.at[block_of(slot)],
            send_sem=down_send.at[peer],
            recv_sem=down_recv.at[slot],
            device_id=(peer, ch),
            device_id_type=MESH,
        )

    def down_start(step, carry):
        peer = (req + step) % REQ
        down_copy(peer, req).start()
        return carry

    lax.fori_loop(1, REQ, down_start, 0)

    def down_drain(step, carry):
        down_copy((req + step) % REQ, req).wait_send()
        return carry

    drains.append(lambda: lax.fori_loop(1, REQ, down_drain, 0))
    down_in[block_of(req), :] = down_out[block_of(req), :]

    def down_wait(step, carry):
        peer = (req + REQ - step) % REQ
        down_copy(peer, peer).wait_recv()
        return carry

    lax.fori_loop(1, REQ, down_wait, 0)
    total = down_in[:BLOCK, :].astype(f32)
    for index in range(1, REQ):
        total = total + down_in[index * BLOCK : (index + 1) * BLOCK, :].astype(f32)
    total = total + own_block[...]
    for row in range(ROWS):
        for chunk in range(CHUNKS):
            spot = row * CHUNKS + place(chunk)
            result[row : row + 1, chunk * LANES : (chunk + 1) * LANES] = total[spot : spot + 1]
    out_ref[...] = result[...].astype(bf16)

    finish()


def fused(
    tokens,
    attn_gain,
    w_query,
    w_keyval,
    cache,
    lengths,
    write_pos,
    w_out,
    mlp_gain,
    w_gate_up,
    w_down,
):
    f32 = jnp.float32
    bf16 = jnp.bfloat16
    window = cache.shape[3]
    pieces = w_down.shape[0] // 256
    every = ROWS * REQ
    vmem = pl.BlockSpec(memory_space=pltpu.VMEM)
    hbm = pl.BlockSpec(memory_space=pltpu.HBM)
    dma = pltpu.SemaphoreType.DMA
    return pl.pallas_call(
        fused_kernel,
        out_shape=(
            jax.ShapeDtypeStruct(tokens.shape, bf16),
            jax.ShapeDtypeStruct((ROWS, 2 * LANES), bf16),
        ),
        in_specs=[hbm] * 11,
        out_specs=(vmem, vmem),
        scratch_shapes=[
            pltpu.VMEM(tokens.shape, bf16),
            pltpu.VMEM((1, attn_gain.shape[0]), f32),
            pltpu.SMEM(lengths.shape, jnp.int32),
            pltpu.SMEM(write_pos.shape, jnp.int32),
            pltpu.VMEM((1, mlp_gain.shape[0]), f32),
            pltpu.VMEM(w_query.shape, bf16),
            pltpu.VMEM(w_keyval.shape[::-1], bf16),
            pltpu.VMEM(cache.shape[1:], bf16),
            pltpu.VMEM(cache.shape[1:], bf16),
            pltpu.VMEM(w_out.shape, bf16),
            pltpu.VMEM(w_gate_up.shape, bf16),
            pltpu.VMEM(w_down.shape, bf16),
            pltpu.VMEM((BLOCK, LANES), f32),
            pltpu.VMEM((3, BLOCK, LANES), bf16),
            pltpu.VMEM((3, REQ * BLOCK, LANES), bf16),
            pltpu.VMEM((3, REQ * BLOCK, LANES), f32),
            pltpu.VMEM((2, REQ * TILE, LANES), f32),
            pltpu.VMEM((2, CH * HALF * TILE, LANES), f32),
            pltpu.VMEM((ROWS, H, window), f32),
            pltpu.VMEM((ROWS, H, window), f32),
            pltpu.VMEM((ROWS, H, LANES), f32),
            pltpu.VMEM((ROWS, H, LANES), f32),
            pltpu.VMEM((every, LANES), f32),
            pltpu.VMEM((every, LANES), f32),
            pltpu.VMEM((pieces, every, 512), f32),
            pltpu.VMEM((pieces, every, 512), bf16),
            pltpu.VMEM((pieces, every, 512), bf16),
            pltpu.VMEM((REQ * BLOCK, LANES), f32),
            pltpu.VMEM((REQ * BLOCK, LANES), bf16),
            pltpu.VMEM((REQ * BLOCK, LANES), bf16),
            pltpu.VMEM(tokens.shape, f32),
            dma((12,)),
            dma((3, REQ)),
            dma((3, REQ)),
            dma((2, REQ)),
            dma((2, CH * HALF)),
            dma((ROWS,)),
            dma((ROWS,)),
            dma((1,)),
            dma((1,)),
            dma((1,)),
            dma((1,)),
            dma((pieces,)),
            dma((pieces,)),
            dma((REQ,)),
            dma((REQ,)),
        ],
        compiler_params=pltpu.CompilerParams(
            collective_id=0, has_side_effects=True, vmem_limit_bytes=60 * 1024 * 1024
        ),
    )(
        tokens,
        attn_gain.reshape(1, -1),
        w_query,
        w_keyval.T,
        cache,
        lengths,
        write_pos,
        w_out,
        mlp_gain.reshape(1, -1),
        w_gate_up,
        w_down,
    )


def solution(mesh):
    placed = (
        P("req", "ch"),
        P("ch"),
        P("ch", "req"),
        P("ch", "req"),
        P(None, "req", "ch", None),
        P("req"),
        P("req"),
        P("ch", "req"),
        P("ch"),
        P("ch", "req"),
        P("req", "ch"),
    )
    def step(*args):
        tokens, cache = args[0], args[4]
        fits = (
            mesh.shape["ch"] == CH
            and mesh.shape["req"] == REQ
            and tokens.shape[0] == ROWS
            and tokens.shape[1] == CHUNKS * LANES
            and cache.shape[2] == LANES
        )
        return (fused if fits else body)(*args)

    return jax.shard_map(
        step,
        mesh=mesh,
        in_specs=placed,
        out_specs=(P("req", "ch"), P("req", "ch")),
        check_vma=False,
    )
```

```python
import math

import jax
import jax.numpy as jnp
from jax import lax
from jax.experimental import pallas as pl
from jax.experimental.pallas import tpu as pltpu
from jax.sharding import PartitionSpec as P

D = 4096
H = 16
HD = 256


EPSILON = 1e-06


def rms_norm(values, gain):
    wide = values.astype(jnp.float32)
    squares = jnp.sum(wide * wide, axis=1)
    summed = lax.psum(squares, "ch")
    meansq = summed / D
    return (wide * lax.rsqrt(meansq + EPSILON)[:, None] * gain[None, :]).astype(jnp.bfloat16)


def body(
    tokens,
    attn_gain,
    w_query,
    w_keyval,
    cache,
    lengths,
    write_pos,
    w_out,
    mlp_gain,
    w_gate_up,
    w_down,
):
    rows = tokens.shape[0]
    chan = cache.shape[2]
    window = cache.shape[3]
    factor = 1.0 / math.sqrt(HD)
    normed = rms_norm(tokens, attn_gain)
    joined = jnp.concatenate([w_query, w_keyval], axis=1)
    head_parts = jnp.dot(
        lax.all_gather(normed, "req", axis=0, tiled=True),
        joined,
        preferred_element_type=jnp.float32,
    )
    query_cols = w_query.shape[1]
    query_part, keyval_part = (
        lax.all_to_all(head_parts[:, :query_cols], "req", split_axis=0, concat_axis=1, tiled=True),
        lax.all_to_all(head_parts[:, query_cols:], "req", split_axis=0, concat_axis=1, tiled=True),
    )
    query_sum, keyval_sum = (
        lax.psum_scatter(query_part, "ch", scatter_dimension=1, tiled=True),
        lax.psum_scatter(keyval_part, "ch", scatter_dimension=1, tiled=True),
    )
    queries = query_sum.astype(jnp.bfloat16).reshape(rows, H, chan)
    keyval_new = keyval_sum.astype(jnp.bfloat16)
    key_new = keyval_new[:, :chan]
    value_new = keyval_new[:, chan:]
    keys = cache[0]
    values_cache = cache[1]
    own_part = jnp.sum(
        queries.astype(jnp.float32) * key_new.astype(jnp.float32)[:, None, :], axis=-1
    )
    score_part = jnp.einsum("bhe,bew->bhw", queries, keys, preferred_element_type=jnp.float32)
    summed, own_sum = lax.psum((score_part, own_part), "ch")
    slot_index = jnp.arange(window, dtype=jnp.int32)
    offset = (write_pos[:, None] - 1 - slot_index[None, :]) % window
    usable = offset < lengths[:, None]
    scores = jnp.where(usable[:, None, :], summed * factor, -jnp.inf)
    own_score = own_sum * factor
    top = jnp.maximum(jnp.max(scores, axis=-1), own_score)
    weights = jnp.exp(scores - top[..., None])
    own_weight = jnp.exp(own_score - top)
    total = jnp.sum(weights, axis=-1) + own_weight
    weights_low = weights.astype(jnp.bfloat16)
    numer = jnp.einsum(
        "bhw,bew->bhe", weights_low, values_cache, preferred_element_type=jnp.float32
    )
    numer = (
        numer
        + own_weight.astype(jnp.bfloat16).astype(jnp.float32)[..., None]
        * value_new.astype(jnp.float32)[:, None, :]
    )
    attn_local = (numer / total[..., None]).astype(jnp.bfloat16).reshape(rows, H * chan)
    out_parts = jnp.dot(
        lax.all_gather(attn_local, "req", axis=0, tiled=True),
        w_out,
        preferred_element_type=jnp.float32,
    )
    out_part = lax.all_to_all(out_parts, "req", split_axis=0, concat_axis=1, tiled=True)
    out_sum = lax.psum_scatter(out_part, "ch", scatter_dimension=1, tiled=True)
    first = (tokens.astype(jnp.float32) + out_sum).astype(jnp.bfloat16)
    normed_two = rms_norm(first, mlp_gain)
    hidden_cols = w_gate_up.shape[1] // 2
    ffn_parts = jnp.dot(
        lax.all_gather(normed_two, "req", axis=0, tiled=True),
        w_gate_up,
        preferred_element_type=jnp.float32,
    )
    ffn_total = lax.psum(ffn_parts, "ch")
    hidden = (
        jax.nn.gelu(ffn_total[:, :hidden_cols], approximate=True) * ffn_total[:, hidden_cols:]
    ).astype(jnp.bfloat16)
    down_sum = lax.psum_scatter(
        jnp.dot(hidden, w_down, preferred_element_type=jnp.float32),
        "req",
        scatter_dimension=0,
        tiled=True,
    )
    layer_out = (first.astype(jnp.float32) + down_sum).astype(jnp.bfloat16)
    return (layer_out, keyval_new)


REQ = 16
CH = 2
ROWS = 2
LANES = 128
CHUNKS = 16
HALF = REQ // CH
BLOCK = ROWS * CHUNKS
TILE = 8
MESH = pl.DeviceIdType.MESH


def place(chunk):
    return (chunk % 2) * HALF + chunk // 2


def fused_kernel(
    tokens_hbm,
    attn_gain_hbm,
    w_query_hbm,
    w_keyval_hbm,
    cache_hbm,
    lengths_hbm,
    write_pos_hbm,
    w_out_hbm,
    mlp_gain_hbm,
    w_gate_up_hbm,
    w_down_hbm,
    out_ref,
    kv_ref,
    tokens_ref,
    attn_gain_ref,
    lengths_ref,
    write_pos_ref,
    mlp_gain_ref,
    w_query,
    w_keyval,
    keys,
    values,
    w_out,
    w_gate_up,
    w_down,
    own_block,
    sends,
    gathered,
    wide,
    parts_out,
    parts_in,
    score_out,
    score_in,
    own_out,
    own_in,
    square_out,
    square_in,
    ffn_own,
    ffn_out,
    ffn_in,
    down_wide,
    down_out,
    down_in,
    result,
    load_sem,
    gather_send,
    gather_recv,
    parts_send,
    parts_recv,
    score_send,
    score_recv,
    own_send,
    own_recv,
    square_send,
    square_recv,
    ffn_send,
    ffn_recv,
    down_send,
    down_recv,
):
    req = lax.axis_index("req")
    ch = lax.axis_index("ch")
    other = 1 - ch
    window = keys.shape[2]
    hidden_cols = w_down.shape[0]
    factor = 1.0 / math.sqrt(HD)
    f32 = jnp.float32
    bf16 = jnp.bfloat16

    drains = []

    def flush(keep):
        ready = drains[: len(drains) - keep]
        del drains[: len(drains) - keep]
        for drain in ready:
            drain()

    def finish():
        flush(0)

    barrier = pltpu.get_barrier_semaphore()
    me = req * CH + ch

    def greet(step, carry):
        peer = (me + step) % (REQ * CH)
        pl.semaphore_signal(barrier, inc=1, device_id=(peer // CH, peer % CH), device_id_type=MESH)
        return carry

    lax.fori_loop(1, REQ * CH, greet, 0, unroll=True)

    loads = [
        pltpu.make_async_copy(src, dst, load_sem.at[index])
        for index, (src, dst) in enumerate(
            (
                (tokens_hbm, tokens_ref),
                (attn_gain_hbm, attn_gain_ref),
                (w_query_hbm, w_query),
                (w_keyval_hbm, w_keyval),
                (lengths_hbm, lengths_ref),
                (write_pos_hbm, write_pos_ref),
                (cache_hbm.at[0], keys),
                (cache_hbm.at[1], values),
                (w_out_hbm, w_out),
                (mlp_gain_hbm, mlp_gain_ref),
                (w_gate_up_hbm, w_gate_up),
                (w_down_hbm, w_down),
            )
        )
    ]
    for load in loads:
        load.start()

    loads[0].wait()
    tokens = tokens_ref[...].astype(f32)
    for row in range(ROWS):
        for chunk in range(CHUNKS):
            spot = row * CHUNKS + place(chunk)
            own_block[spot : spot + 1, :] = tokens[row : row + 1, chunk * LANES : (chunk + 1) * LANES]

    pl.semaphore_wait(barrier, REQ * CH - 1)

    def block_of(index):
        return pl.ds(pl.multiple_of(index * BLOCK, BLOCK), BLOCK)

    def tile_of(index):
        return pl.ds(pl.multiple_of(index * TILE, TILE), TILE)

    def gather_copy(phase, peer, slot):
        return pltpu.make_async_remote_copy(
            src_ref=sends.at[phase],
            dst_ref=gathered.at[phase, block_of(slot)],
            send_sem=gather_send.at[phase, peer],
            recv_sem=gather_recv.at[phase, slot],
            device_id=(peer, ch),
            device_id_type=MESH,
        )

    def gather(phase, block):
        sends[phase] = block
        gathered[phase, block_of(req), :] = block

        def start(step, carry):
            peer = (req + step) % REQ
            gather_copy(phase, peer, req).start()
            return carry

        lax.fori_loop(1, REQ, start, 0, unroll=True)

        def drain(step, carry):
            gather_copy(phase, (req + step) % REQ, req).wait_send()
            return carry

        drains.append(lambda: lax.fori_loop(1, REQ, drain, 0, unroll=True))

    def gather_wait(phase):
        flush(1)

        def wait(step, carry):
            peer = (req + REQ - step) % REQ
            gather_copy(phase, peer, peer).wait_recv()
            return carry

        lax.fori_loop(1, REQ, wait, 0, unroll=True)
        wide[phase] = gathered[phase].astype(f32)

    def chunk_rows(phase, chunk):
        spot = place(chunk)
        return jnp.concatenate(
            [wide[phase, pl.ds(row * CHUNKS + spot, REQ, stride=BLOCK), :] for row in range(ROWS)],
            axis=0,
        )

    def gained(phase, gain_ref):
        total = None
        pieces = []
        for chunk in range(CHUNKS):
            piece = chunk_rows(phase, chunk)
            square = piece * piece
            total = square if total is None else total + square
            pieces.append((piece * gain_ref[:, chunk * LANES : (chunk + 1) * LANES]).astype(bf16))
        return jnp.concatenate(pieces, axis=1), jnp.sum(total, axis=1, keepdims=True)

    def parts_copy(phase, peer, slot):
        return pltpu.make_async_remote_copy(
            src_ref=parts_out.at[phase, tile_of(peer)],
            dst_ref=parts_in.at[phase, tile_of(slot)],
            send_sem=parts_send.at[phase, peer],
            recv_sem=parts_recv.at[phase, slot],
            device_id=(peer, req // HALF),
            device_id_type=MESH,
        )

    my_slot = ch * HALF + req % HALF

    def is_self(peer):
        return jnp.logical_and(peer == req, req // HALF == ch)

    def scatter(phase, rows):
        for index, piece in enumerate(rows):
            parts_out[phase, pl.ds(index, REQ, stride=TILE), :] = piece

        def start(step, carry):
            peer = (req + step) % REQ

            @pl.when(jnp.logical_not(is_self(peer)))
            def _():
                parts_copy(phase, peer, my_slot).start()

            return carry

        lax.fori_loop(0, REQ, start, 0, unroll=True)

        def drain(peer, carry):
            @pl.when(jnp.logical_not(is_self(peer)))
            def _():
                parts_copy(phase, peer, my_slot).wait_send()

            return carry

        drains.append(lambda: lax.fori_loop(0, REQ, drain, 0, unroll=True))

        @pl.when(req // HALF == ch)
        def _():
            parts_in[phase, tile_of(my_slot), :] = parts_out[phase, tile_of(req), :]

    def scatter_wait(phase):
        flush(1)

        def wait(slot, carry):
            mine = jnp.logical_and(slot == my_slot, req // HALF == ch)

            @pl.when(jnp.logical_not(mine))
            def _():
                parts_copy(phase, req, slot).wait_recv()

            return carry

        lax.fori_loop(0, CH * HALF, wait, 0, unroll=True)

    def summed(phase, index):
        pieces = parts_in[phase, pl.ds(index, CH * HALF, stride=TILE), :]
        return pieces[:HALF] + pieces[HALF:]

    gather(0, own_block[...].astype(bf16))
    for load in loads[1:4]:
        load.wait()
    gather_wait(0)
    lhs, squares = gained(0, attn_gain_ref)
    query_part = jnp.dot(lhs, w_query[...], preferred_element_type=f32)
    keyval_part = lax.dot_general(
        lhs, w_keyval[...], (((1,), (1,)), ((), ())), preferred_element_type=f32
    )
    per_row = LANES // keyval_part.shape[1]
    lane = lax.broadcasted_iota(jnp.int32, (ROWS * REQ, LANES), 1)
    keyval_part = jnp.where(
        lane // keyval_part.shape[1] == req % per_row,
        jnp.concatenate([keyval_part] * per_row, axis=1),
        0.0,
    )
    squares = jnp.broadcast_to(squares, (ROWS * REQ, LANES))

    def by_row(array):
        return [array[row * REQ : (row + 1) * REQ] for row in range(ROWS)]

    scatter(
        0,
        by_row(query_part[:, :LANES])
        + by_row(query_part[:, LANES:])
        + by_row(keyval_part)
        + by_row(squares),
    )
    for load in loads[4:7]:
        load.wait()
    scatter_wait(0)

    def score_copy(row):
        return pltpu.make_async_remote_copy(
            src_ref=score_out.at[row],
            dst_ref=score_in.at[row],
            send_sem=score_send.at[row],
            recv_sem=score_recv.at[row],
            device_id=(req, other),
            device_id_type=MESH,
        )

    own_copy = pltpu.make_async_remote_copy(
        src_ref=own_out,
        dst_ref=own_in,
        send_sem=own_send.at[0],
        recv_sem=own_recv.at[0],
        device_id=(req, other),
        device_id_type=MESH,
    )
    values_new = []
    for row in range(ROWS):
        scale = lax.rsqrt(summed(0, 6 + row)[:1, :] / D + EPSILON)
        query = (jnp.concatenate([summed(0, row), summed(0, 2 + row)], axis=0) * scale).astype(bf16)
        score_out[row] = jnp.dot(query, keys[row], preferred_element_type=f32)
        score_copy(row).start()
        drains.append(score_copy(row).wait_send)
        keyval = summed(0, 4 + row) * scale
        key_new = jnp.sum(keyval[: HALF // 2], axis=0, keepdims=True).astype(bf16)
        value_new = jnp.sum(keyval[HALF // 2 :], axis=0, keepdims=True).astype(bf16)
        own = jnp.sum(query.astype(f32) * key_new.astype(f32), axis=1, keepdims=True)
        own_out[row] = jnp.broadcast_to(own, (H, LANES))
        values_new.append(value_new.astype(f32))
        result[row : row + 1, :LANES] = key_new.astype(f32)
        result[row : row + 1, LANES : 2 * LANES] = value_new.astype(f32)
    own_copy.start()
    drains.append(own_copy.wait_send)
    kv_ref[...] = result[:, : 2 * LANES].astype(bf16)
    loads[7].wait()
    flush(ROWS + 1)
    mixed = []
    slot_index = lax.broadcasted_iota(jnp.int32, (H, window), 1)
    for row in range(ROWS):
        score_copy(row).wait_recv()
        if row == 0:
            own_copy.wait_recv()
        offset = write_pos_ref[row] - 1 - slot_index
        offset = jnp.where(offset < 0, offset + window, offset)
        scores = jnp.where(
            offset < lengths_ref[row], (score_out[row] + score_in[row]) * factor, -jnp.inf
        )
        own = (own_out[row] + own_in[row])[:, :1] * factor
        top = jnp.maximum(jnp.max(scores, axis=1, keepdims=True), own)
        weights = jnp.exp(scores - top)
        own_weight = jnp.exp(own - top)
        total = jnp.sum(weights, axis=1, keepdims=True) + own_weight
        numer = lax.dot_general(
            weights.astype(bf16), values[row], (((1,), (1,)), ((), ())), preferred_element_type=f32
        )
        numer = numer + own_weight.astype(bf16).astype(f32) * values_new[row]
        mixed.append(numer / total)

    gather(1, jnp.concatenate(mixed, axis=0).astype(bf16))
    loads[8].wait()
    gather_wait(1)
    lhs = jnp.concatenate([chunk_rows(1, chunk) for chunk in range(CHUNKS)], axis=1).astype(bf16)
    out_part = jnp.dot(lhs, w_out[...], preferred_element_type=f32)
    scatter(1, by_row(out_part[:, :LANES]) + by_row(out_part[:, LANES:]))
    scatter_wait(1)
    first = jnp.concatenate(
        [piece for row in range(ROWS) for piece in (summed(1, row), summed(1, 2 + row))], axis=0
    )
    first = (own_block[...] + first).astype(bf16)
    own_block[...] = first.astype(f32)

    gather(2, first)
    for load in loads[9:]:
        load.wait()
    gather_wait(2)
    lhs, squares = gained(2, mlp_gain_ref)
    square_out[...] = jnp.broadcast_to(squares, (ROWS * REQ, LANES))
    square_copy = pltpu.make_async_remote_copy(
        src_ref=square_out,
        dst_ref=square_in,
        send_sem=square_send.at[0],
        recv_sem=square_recv.at[0],
        device_id=(req, other),
        device_id_type=MESH,
    )
    square_copy.start()
    drains.append(square_copy.wait_send)
    pieces, _, double = ffn_own.shape
    width = double // 2

    def ffn_copy(piece):
        return pltpu.make_async_remote_copy(
            src_ref=ffn_out.at[piece],
            dst_ref=ffn_in.at[piece],
            send_sem=ffn_send.at[piece],
            recv_sem=ffn_recv.at[piece],
            device_id=(req, other),
            device_id_type=MESH,
        )

    for piece in range(pieces):
        for part in range(2):
            begin = part * hidden_cols + piece * width
            block = jnp.dot(lhs, w_gate_up[:, begin : begin + width], preferred_element_type=f32)
            ffn_own[piece, :, part * width : (part + 1) * width] = block
            ffn_out[piece, :, part * width : (part + 1) * width] = block.astype(bf16)
        ffn_copy(piece).start()
        drains.append(ffn_copy(piece).wait_send)
    flush(pieces + 1)
    square_copy.wait_recv()
    scale = lax.rsqrt((square_out[...] + square_in[...])[:, :1] / D + EPSILON)
    down = None
    for piece in range(pieces):
        ffn_copy(piece).wait_recv()
        both = (ffn_own[piece] + ffn_in[piece].astype(f32)) * scale
        hidden = (jax.nn.gelu(both[:, :width], approximate=True) * both[:, width:]).astype(bf16)
        term = jnp.dot(
            hidden, w_down[piece * width : (piece + 1) * width, :], preferred_element_type=f32
        )
        down = term if down is None else down + term

    for chunk in range(CHUNKS):
        columns = down[:, chunk * LANES : (chunk + 1) * LANES]
        for row in range(ROWS):
            down_wide[pl.ds(row * CHUNKS + place(chunk), REQ, stride=BLOCK), :] = columns[
                row * REQ : (row + 1) * REQ
            ]
    down_out[...] = down_wide[...].astype(bf16)

    def down_copy(peer, slot):
        return pltpu.make_async_remote_copy(
            src_ref=down_out.at[block_of(peer)],
            dst_ref=down_in.at[block_of(slot)],
            send_sem=down_send.at[peer],
            recv_sem=down_recv.at[slot],
            device_id=(peer, ch),
            device_id_type=MESH,
        )

    def down_start(step, carry):
        peer = (req + step) % REQ
        down_copy(peer, req).start()
        return carry

    lax.fori_loop(1, REQ, down_start, 0, unroll=True)

    def down_drain(step, carry):
        down_copy((req + step) % REQ, req).wait_send()
        return carry

    drains.append(lambda: lax.fori_loop(1, REQ, down_drain, 0, unroll=True))
    down_in[block_of(req), :] = down_out[block_of(req), :]

    flush(1)

    def down_wait(step, carry):
        peer = (req + REQ - step) % REQ
        down_copy(peer, peer).wait_recv()
        return carry

    lax.fori_loop(1, REQ, down_wait, 0, unroll=True)
    total = down_in[:BLOCK, :].astype(f32)
    for index in range(1, REQ):
        total = total + down_in[index * BLOCK : (index + 1) * BLOCK, :].astype(f32)
    total = total + own_block[...]
    for row in range(ROWS):
        for chunk in range(CHUNKS):
            spot = row * CHUNKS + place(chunk)
            result[row : row + 1, chunk * LANES : (chunk + 1) * LANES] = total[spot : spot + 1]
    out_ref[...] = result[...].astype(bf16)

    finish()


def fused(
    tokens,
    attn_gain,
    w_query,
    w_keyval,
    cache,
    lengths,
    write_pos,
    w_out,
    mlp_gain,
    w_gate_up,
    w_down,
):
    f32 = jnp.float32
    bf16 = jnp.bfloat16
    window = cache.shape[3]
    pieces = w_down.shape[0] // 256
    every = ROWS * REQ
    vmem = pl.BlockSpec(memory_space=pltpu.VMEM)
    hbm = pl.BlockSpec(memory_space=pltpu.HBM)
    dma = pltpu.SemaphoreType.DMA
    return pl.pallas_call(
        fused_kernel,
        out_shape=(
            jax.ShapeDtypeStruct(tokens.shape, bf16),
            jax.ShapeDtypeStruct((ROWS, 2 * LANES), bf16),
        ),
        in_specs=[hbm] * 11,
        out_specs=(vmem, vmem),
        scratch_shapes=[
            pltpu.VMEM(tokens.shape, bf16),
            pltpu.VMEM((1, attn_gain.shape[0]), f32),
            pltpu.SMEM(lengths.shape, jnp.int32),
            pltpu.SMEM(write_pos.shape, jnp.int32),
            pltpu.VMEM((1, mlp_gain.shape[0]), f32),
            pltpu.VMEM(w_query.shape, bf16),
            pltpu.VMEM(w_keyval.shape[::-1], bf16),
            pltpu.VMEM(cache.shape[1:], bf16),
            pltpu.VMEM(cache.shape[1:], bf16),
            pltpu.VMEM(w_out.shape, bf16),
            pltpu.VMEM(w_gate_up.shape, bf16),
            pltpu.VMEM(w_down.shape, bf16),
            pltpu.VMEM((BLOCK, LANES), f32),
            pltpu.VMEM((3, BLOCK, LANES), bf16),
            pltpu.VMEM((3, REQ * BLOCK, LANES), bf16),
            pltpu.VMEM((3, REQ * BLOCK, LANES), f32),
            pltpu.VMEM((2, REQ * TILE, LANES), f32),
            pltpu.VMEM((2, CH * HALF * TILE, LANES), f32),
            pltpu.VMEM((ROWS, H, window), f32),
            pltpu.VMEM((ROWS, H, window), f32),
            pltpu.VMEM((ROWS, H, LANES), f32),
            pltpu.VMEM((ROWS, H, LANES), f32),
            pltpu.VMEM((every, LANES), f32),
            pltpu.VMEM((every, LANES), f32),
            pltpu.VMEM((pieces, every, 512), f32),
            pltpu.VMEM((pieces, every, 512), bf16),
            pltpu.VMEM((pieces, every, 512), bf16),
            pltpu.VMEM((REQ * BLOCK, LANES), f32),
            pltpu.VMEM((REQ * BLOCK, LANES), bf16),
            pltpu.VMEM((REQ * BLOCK, LANES), bf16),
            pltpu.VMEM(tokens.shape, f32),
            dma((12,)),
            dma((3, REQ)),
            dma((3, REQ)),
            dma((2, REQ)),
            dma((2, CH * HALF)),
            dma((ROWS,)),
            dma((ROWS,)),
            dma((1,)),
            dma((1,)),
            dma((1,)),
            dma((1,)),
            dma((pieces,)),
            dma((pieces,)),
            dma((REQ,)),
            dma((REQ,)),
        ],
        compiler_params=pltpu.CompilerParams(
            collective_id=0, has_side_effects=True, vmem_limit_bytes=60 * 1024 * 1024
        ),
    )(
        tokens,
        attn_gain.reshape(1, -1),
        w_query,
        w_keyval.T,
        cache,
        lengths,
        write_pos,
        w_out,
        mlp_gain.reshape(1, -1),
        w_gate_up,
        w_down,
    )


def solution(mesh):
    placed = (
        P("req", "ch"),
        P("ch"),
        P("ch", "req"),
        P("ch", "req"),
        P(None, "req", "ch", None),
        P("req"),
        P("req"),
        P("ch", "req"),
        P("ch"),
        P("ch", "req"),
        P("req", "ch"),
    )
    def step(*args):
        tokens, cache = args[0], args[4]
        fits = (
            mesh.shape["ch"] == CH
            and mesh.shape["req"] == REQ
            and tokens.shape[0] == ROWS
            and tokens.shape[1] == CHUNKS * LANES
            and cache.shape[2] == LANES
        )
        return (fused if fits else body)(*args)

    return jax.shard_map(
        step,
        mesh=mesh,
        in_specs=placed,
        out_specs=(P("req", "ch"), P("req", "ch")),
        check_vma=False,
    )
```
